32 devices in a mesh: dp: 8 (over z, y), expert: 2 (over core), tensor: 2 (over x).
Axes of the slice: x: 2, y: 2, z: 4, core: 2. Of those that a mesh axis runs over, the one named last changes fastest.
Arguments:
- tokens: bfloat16 [16384, 768], P(('dp', 'expert'), 'tensor'), may hold values from -6 to 6
- gain_attn: float32 [768], replicated, may hold values from 0.5 to 1.5
- w_query: bfloat16 [768, 768], P(None, 'tensor'), may hold values from -0.21875 to 0.21875
- w_key: bfloat16 [768, 768], P(None, 'tensor'), may hold values from -0.21875 to 0.21875
- w_value: bfloat16 [768, 768], P(None, 'tensor'), may hold values from -0.21875 to 0.21875
- w_output: bfloat16 [768, 768], P('tensor'), may hold values from -1.75 to 1.75
- gain_moe: float32 [768], replicated, may hold values from 0.5 to 1.5
- w_router: bfloat16 [768, 8], replicated, may hold values from -0.14941406 to 0.14941406
- w_in: bfloat16 [8, 768, 3072], P('expert', None, 'tensor'), may hold values from -0.21875 to 0.21875
- w_out: bfloat16 [8, 3072, 768], P('expert', 'tensor'), may hold values from -0.109375 to 0.109375
- routes: int32 [16384, 2], P(('dp', 'expert')), may hold values from 0 to 7, all different within a row; in each aligned block of 1024 rows (0 to 1023, 1024 to 2047, ...) at most 320 rows name the same one
- cotangent: bfloat16 [16384, 768], P(('dp', 'expert'), 'tensor'), may hold values from -6 to 6
Outputs:
- mixed: bfloat16 [16384, 768], P(('dp', 'expert'), 'tensor')
- grad_tokens: float32 [16384, 768], P(('dp', 'expert'), 'tensor')
- grad_gain_attn: float32 [768], P('tensor')
- grad_query: float32 [768, 768], P(None, 'tensor')
- grad_key: float32 [768, 768], P(None, 'tensor')
- grad_value: float32 [768, 768], P(None, 'tensor')
- grad_output: float32 [768, 768], P('tensor')
- grad_gain_moe: float32 [768], replicated
- grad_router: float32 [768, 8], replicated
- grad_in: float32 [8, 768, 3072], P('expert', 'dp', 'tensor')
- grad_out: float32 [8, 3072, 768], P('expert', 'tensor', 'dp')
The draws below stay inside these ranges and needn't reach their ends.
Inputs may be any that keep to these rules, and one draw needn't show every extreme that they name: `routes`: each row names 2 different experts. In each aligned block of 1024 rows (one sequence) no expert is named by more than 320 rows, a bound that some block reaches.
All inputs are finite; a program needn't handle non-finite values.
Results may differ from the reference program's by a relative error of at most 0.015.
Values may be sent and summed in bfloat16 or wider, within the bound.
A program may use at most 256 MiB of HBM per device.

```python
import math
import jax
import jax.numpy as jnp
import numpy as np
from jax import lax

D = 768
HEADS = 12
DH = 64
FF = 3072
TOP = 2
SEQ = 1024
EXPERTS = 8
CAP = 320
TOKENS = 16384
N_DP = 8
N_EXPERT = 2


def shard_levels(rng, dims, split, smallest, high):
    level = 1.0
    for axis_at, blocks in split:
        heights = jax.random.uniform(jax.random.fold_in(jax.random.fold_in(rng, 6), axis_at), (blocks,), jnp.float32, smallest / len(split), high / len(split))
        level = level * jnp.repeat(jnp.exp(heights), dims[axis_at] // blocks).reshape((-1,) + (1,) * (len(dims) - 1 - axis_at))
    return level


def deal_out(stream_key, own, number, rows, number_of, top, most, lean):
    sequence = jax.random.permutation(stream_key, number_of)
    crowded, ordinary = shares(number_of, rows * top, most, lean, True), shares(number_of, rows * top, most, lean, False)
    places = jnp.arange(number_of)

    def named(lengths, turn):
        used = int((lengths > 0).sum())
        fixed = max(1, used // 4)
        moved = fixed + (places - fixed + turn * (used - fixed)) % max(1, number_of - fixed)
        return jnp.zeros((number_of,), jnp.int32).at[sequence[jnp.where(places < fixed, places, moved)]].set(jnp.asarray(lengths, jnp.int32))

    lengths = jnp.where(number % 4 == 0, named(crowded, number // 4), named(ordinary, number - number // 4 - 1))
    mixed = jax.random.permutation(jax.random.fold_in(own, 3), number_of)
    source_of, taker = mixed[0:number_of // 2 * 2:2], mixed[1:number_of // 2 * 2:2]
    slack = jnp.minimum(lengths[source_of] - 1, most - lengths[taker]) // 2
    slack = jnp.where((source_of == sequence[0]) | (taker == sequence[0]) | (lengths[taker] == 0), 0, jnp.maximum(slack, 0))
    moved = jax.random.randint(jax.random.fold_in(own, 4), (number_of // 2,), 0, 1 << 20) % (slack + 1)
    lengths = lengths.at[source_of].add(-moved).at[taker].add(moved)
    labels = jnp.searchsorted(jnp.cumsum(lengths), jnp.arange(rows * top), side="right").astype(jnp.int32)
    table = labels.reshape(top, rows).T
    table = table[jax.random.permutation(jax.random.fold_in(own, 1), rows)]
    turn = jax.random.randint(jax.random.fold_in(own, 2), (rows, 1), 0, top)
    return jnp.take_along_axis(table, (jnp.arange(top)[None, :] + turn) % top, axis=1)


def shares(amount, total, reach, skew, full):
    portions = [(1 << 20) // math.isqrt(rank ** skew) + 1 for rank in range(1, amount + 1)]
    largest = reach if full else min(reach, max(-(-total // amount), total * portions[0] // sum(portions)))
    least = 1 if total - largest >= amount - 1 else 0
    holding, rest = [largest] + [least] * (amount - 1), total - largest - least * (amount - 1)
    while rest > 0:
        movable = [i for i in range(1, amount) if holding[i] < largest] or [i for i in range(1, amount) if holding[i] < reach]
        whole, left = sum([portions[i] for i in movable]), rest
        for i in movable:
            addition = min(reach - holding[i], max(1, left * portions[i] // whole), rest)
            holding[i] = holding[i] + addition
            rest = rest - addition
    return np.array(holding)


def bell_draw(key, extent, scale, bound, cuts=(), kind=jnp.bfloat16):
    level = shard_levels(key, extent, cuts, -0.22, 0.18) if cuts else 1.0
    values = jax.random.normal(key, extent, jnp.float32) * scale * level
    return jnp.minimum(jnp.maximum(values, -bound), bound).astype(kind)


def setup_inputs(seed: int = 0) -> dict:
    keys = jax.random.split(jax.random.key(seed), 13)
    tokens = bell_draw(keys[0], (TOKENS, D), 1.0, 6.0, ((0, 16), (1, 2)))
    gain_attn = jnp.clip(1.0 + 0.1 * jax.random.normal(keys[1], (D,), jnp.float32), 0.5, 1.5)
    w_query = bell_draw(keys[2], (D, HEADS * DH), D ** -0.5, 0.21875, ((1, 2),))
    w_key = bell_draw(keys[3], (D, HEADS * DH), D ** -0.5, 0.21875, ((1, 2),))
    w_value = bell_draw(keys[4], (D, HEADS * DH), D ** -0.5, 0.21875, ((1, 2),))
    w_output = bell_draw(keys[5], (HEADS * DH, D), (HEADS * DH // 64) ** -0.5, 1.75, ((0, 2),))
    gain_moe = jnp.clip(1.0 + 0.1 * jax.random.normal(keys[6], (D,), jnp.float32), 0.5, 1.5)
    w_router = bell_draw(keys[7], (D, EXPERTS), 0.025, 0.14941406)
    w_in = bell_draw(keys[8], (EXPERTS, D, FF), D ** -0.5, 0.21875, ((0, 2), (2, 2)))
    w_out = bell_draw(keys[9], (EXPERTS, FF, D), FF ** -0.5, 0.109375, ((0, 2), (1, 2)))
    routes_keys = jax.random.split(jax.random.fold_in(keys[10], 1), TOKENS // SEQ)
    routes_turns = jax.random.permutation(jax.random.fold_in(keys[10], 3), TOKENS // SEQ)
    routes = jax.vmap(lambda own, number: deal_out(jax.random.fold_in(keys[10], 2), own, number, SEQ, EXPERTS, TOP, CAP, 2))(routes_keys, routes_turns).reshape((TOKENS, TOP))
    cotangent = bell_draw(keys[11], (TOKENS, D), 1.0, 6.0, ((0, 16), (1, 2)))
    return {"tokens": tokens, "gain_attn": gain_attn, "w_query": w_query, "w_key": w_key, "w_value": w_value, "w_output": w_output, "gain_moe": gain_moe, "w_router": w_router, "w_in": w_in, "w_out": w_out, "routes": routes, "cotangent": cotangent}


@jax.custom_vjp
def low(v):
    return lax.optimization_barrier(v.astype(jnp.bfloat16)).astype(jnp.float32)

@jax.custom_vjp
def low_back(v):
    return v

def low_keep(v):
    return (low(v), None)

def low_pass(kept, grad):
    return (grad,)

def back_keep(v):
    return (v, None)

def back_low(kept, grad):
    return (low(grad),)
low.defvjp(low_keep, low_pass)
low_back.defvjp(back_keep, back_low)
epsilon = 1e-06
highest = lax.Precision.HIGHEST

def matmul(left, right):
    return jnp.dot(left, right, precision=highest)

def rms_norm(rows, gain):
    return rows * lax.rsqrt(lax.optimization_barrier(jnp.mean(rows * rows, axis=-1, keepdims=True)) + epsilon) * gain

def slot_index(routes, experts, capacity):
    flat = routes.reshape(-1).astype(jnp.int32)
    onehot = (flat[:, None] == jnp.arange(experts, dtype=jnp.int32)[None, :]).astype(jnp.int32)
    before = jnp.cumsum(onehot, axis=0) - onehot
    position = lax.optimization_barrier(jnp.sum(before * onehot, axis=1)).astype(jnp.int32)
    return (flat * capacity + position).astype(jnp.int32)

def attention(normed, w_query, w_key, w_value, w_output):
    seq_len = normed.shape[0]
    query = low(low_back(matmul(normed, w_query))).reshape(seq_len, HEADS, DH)
    key_rows = low(low_back(matmul(normed, w_key))).reshape(seq_len, HEADS, DH)
    value_rows = low(low_back(matmul(normed, w_value))).reshape(seq_len, HEADS, DH)
    block = min(512, seq_len)
    factor = 1.0 / math.sqrt(DH)

    def attend(index):
        start = (index * block).astype(jnp.int32)
        query_block = lax.dynamic_slice_in_dim(query, start, block, 0)
        scores = low_back(jnp.einsum('qhd,khd->hqk', query_block, key_rows, precision=highest) * factor)
        rows_at = start + jnp.arange(block, dtype=jnp.int32)[:, None]
        cols_at = jnp.arange(seq_len, dtype=jnp.int32)[None, :]
        scores = jnp.where(cols_at <= rows_at, scores, -1e+30)
        peak = lax.optimization_barrier(jnp.max(scores, axis=-1, keepdims=True))
        expo = jnp.exp(scores - peak)
        prob = low(expo / lax.optimization_barrier(jnp.sum(expo, axis=-1, keepdims=True)))
        return jnp.einsum('hqk,khd->qhd', prob, value_rows, precision=highest)
    blocks = lax.map(jax.checkpoint(attend), jnp.arange(seq_len // block, dtype=jnp.int32))
    heads_out = low(low_back(blocks.reshape(seq_len, HEADS * DH)))
    return low_back(matmul(heads_out, w_output))

def layer(rows, gain_attn, w_query, w_key, w_value, w_output, gain_moe, w_router, w_in, w_out, routes):
    normed_one = low(rms_norm(rows, gain_attn))
    hidden = rows + attention(normed_one, w_query, w_key, w_value, w_output)
    normed_two = low(rms_norm(hidden, gain_moe))
    logits = matmul(normed_two, w_router)
    picks = (routes[:, :, None] == jnp.arange(EXPERTS, dtype=jnp.int32)[None, None, :]).astype(logits.dtype)
    chosen = jnp.einsum('ske,se->sk', picks, logits, precision=highest)
    peak = lax.optimization_barrier(jnp.max(chosen, axis=1, keepdims=True))
    expo = jnp.exp(chosen - peak)
    gates = expo / lax.optimization_barrier(jnp.sum(expo, axis=1, keepdims=True))
    place = slot_index(routes, EXPERTS, CAP)
    doubled = jnp.repeat(normed_two, TOP, axis=0)
    send = jnp.zeros((EXPERTS * CAP, D), normed_two.dtype).at[place].set(doubled).reshape(EXPERTS, CAP, D)
    pre = low_back(jnp.einsum('ecd,edf->ecf', send, w_in, precision=highest))
    active = low(jax.nn.gelu(pre))
    expert_rows = low_back(jnp.einsum('ecf,efd->ecd', active, w_out, precision=highest))
    kept = expert_rows.reshape(EXPERTS * CAP, D)[place].reshape(-1, TOP, D)
    return hidden + lax.optimization_barrier(jnp.sum(gates[:, :, None] * kept, axis=1))

def reference(tokens, gain_attn, w_query, w_key, w_value, w_output, gain_moe, w_router, w_in, w_out, routes, cotangent):
    weights = tuple((w.astype(jnp.float32) for w in (gain_attn, w_query, w_key, w_value, w_output, gain_moe, w_router, w_in, w_out)))
    groups = N_DP * N_EXPERT
    rows_all = tokens.astype(jnp.float32).reshape(groups, SEQ, D)
    cot_all = cotangent.astype(jnp.float32).reshape(groups, SEQ, D)
    route_all = routes.reshape(groups, SEQ, TOP)

    def step(totals, item):
        rows, cot, route_rows = item

        def forward(rows, *params):
            return layer(rows, *params, route_rows)
        result, pull = jax.vjp(forward, rows, *weights)
        grads = pull(cot)
        return (tuple((a + b for a, b in zip(totals, grads[1:]))), (result, grads[0]))
    zeros = tuple((jnp.zeros_like(w) for w in weights))
    totals, (results, grad_rows) = lax.scan(step, zeros, (rows_all, cot_all, route_all))
    return (results.reshape(-1, D).astype(jnp.bfloat16), grad_rows.reshape(-1, D), totals[0], totals[1], totals[2], totals[3], totals[4], totals[5], totals[6], totals[7], totals[8])
```

```python
import functools
import math

import jax
import jax.numpy as jnp
from jax import lax
from jax.experimental import pallas as pl
from jax.experimental.pallas import tpu as pltpu
from jax.sharding import PartitionSpec as P

D = 768
DH = 64
TOP = 2
epsilon = 1e-06
bf16 = jnp.bfloat16
f32 = jnp.float32
FACTOR = 1.0 / math.sqrt(DH)
QB = 256
CHUNK = 768
ROOT = math.sqrt(2.0 / math.pi)
CUBE = 0.044715


def rms_scale(rows):
    return lax.rsqrt(jnp.mean(rows * rows, axis=-1, keepdims=True) + epsilon)


def dot(a, b, ca=1, cb=0):
    return lax.dot_general(a, b, (((ca,), (cb,)), ((), ())), preferred_element_type=f32)


def causal(rows, cols, start):
    at = start + lax.broadcasted_iota(jnp.int32, (rows, cols), 0)
    return lax.broadcasted_iota(jnp.int32, (rows, cols), 1) <= at


def attend_kernel(q_ref, k_ref, v_ref, o_ref, l_ref):
    seq = q_ref.shape[0]
    for half in range(2):
        cols = slice(half * DH, half * DH + DH)
        for start in range(0, seq, QB):
            end = start + QB
            s = dot(q_ref[start:end, cols], k_ref[:end, cols], 1, 1) * FACTOR
            s = jnp.where(causal(QB, end, start), s, -1e30)
            peak = jnp.max(s, axis=1, keepdims=True)
            expo = jnp.exp(s - peak)
            total = jnp.sum(expo, axis=1, keepdims=True)
            prob = (expo * (1.0 / total)).astype(bf16)
            o_ref[start:end, cols] = dot(prob, v_ref[:end, cols]).astype(bf16)
            l_ref[start:end, cols] = jnp.broadcast_to(peak + jnp.log(total), (QB, DH))


def attend(query, key, value):
    seq, width = query.shape
    spec = pl.BlockSpec((seq, 128), lambda i: (0, i))
    return pl.pallas_call(
        attend_kernel,
        grid=(width // 128,),
        in_specs=[spec] * 3,
        out_specs=[spec] * 2,
        out_shape=[
            jax.ShapeDtypeStruct((seq, width), bf16),
            jax.ShapeDtypeStruct((seq, width), f32),
        ],
        compiler_params=pltpu.CompilerParams(vmem_limit_bytes=48 << 20),
    )(query, key, value)


def back_kernel(q_ref, k_ref, v_ref, o_ref, l_ref, g_ref, dq_ref, dk_ref, dv_ref, ks, vs):
    seq = q_ref.shape[0]
    for half in range(2):
        cols = slice(half * DH, half * DH + DH)
        ks[...] = jnp.zeros_like(ks)
        vs[...] = jnp.zeros_like(vs)
        for start in range(0, seq, QB):
            end = start + QB
            q = q_ref[start:end, cols]
            k = k_ref[:end, cols]
            g = g_ref[start:end, cols]
            s = dot(q, k, 1, 1) * FACTOR
            log_total = l_ref[start:end, half * DH : half * DH + 1]
            prob = jnp.where(causal(QB, end, start), jnp.exp(s - log_total), 0.0)
            gp = dot(g, v_ref[:end, cols], 1, 1)
            inner = jnp.sum(
                g.astype(f32) * o_ref[start:end, cols].astype(f32), axis=1, keepdims=True
            )
            ds = (prob * (gp - inner)).astype(bf16)
            dq_ref[start:end, cols] = (dot(ds, k) * FACTOR).astype(bf16)
            ks[:end] += dot(ds, q, 0, 0)
            vs[:end] += dot(prob.astype(bf16), g, 0, 0)
        dk_ref[:, cols] = (ks[...] * FACTOR).astype(bf16)
        dv_ref[:, cols] = vs[...].astype(bf16)


def attend_back(query, key, value, out, log_total, grad):
    seq, width = query.shape
    spec = pl.BlockSpec((seq, 128), lambda i: (0, i))
    return pl.pallas_call(
        back_kernel,
        grid=(width // 128,),
        in_specs=[spec] * 6,
        out_specs=[spec] * 3,
        out_shape=[jax.ShapeDtypeStruct((seq, width), bf16)] * 3,
        scratch_shapes=[pltpu.VMEM((seq, DH), f32)] * 2,
        compiler_params=pltpu.CompilerParams(vmem_limit_bytes=48 << 20),
    )(query, key, value, out, log_total, grad)


def moe_kernel(
    cap,
    x_ref, dy_ref, pos_ref, gate_ref, wi_ref, wo_ref,
    y_ref, dx_ref, dg_ref, gi_ref, go_ref,
    pick, xin, din, gdin, gcol, eo, dxin,
):
    expert, chunk = pl.program_id(0), pl.program_id(1)
    seq = x_ref.shape[1]

    @pl.when((expert == 0) & (chunk == 0))
    def _():
        y_ref[...] = jnp.zeros_like(y_ref)
        dx_ref[...] = jnp.zeros_like(dx_ref)

    @pl.when(chunk == 0)
    def _():
        dg_ref[...] = jnp.zeros_like(dg_ref)
        eo[...] = jnp.zeros_like(eo)
        dxin[...] = jnp.zeros_like(dxin)
        for s in range(2):
            rows = slice(s * cap, s * cap + cap)
            hit = lax.broadcasted_iota(jnp.int32, (cap, seq), 0) == pos_ref[0, s : s + 1, :]
            gates = jnp.sum(
                jnp.where(hit, gate_ref[0, s : s + 1, :], 0.0), axis=1, keepdims=True
            )
            gcol[rows] = jnp.broadcast_to(gates, (cap, 128))
            mask = jnp.where(hit, 1.0, 0.0).astype(bf16)
            pick[rows] = mask
            xin[rows] = dot(mask, x_ref[s]).astype(bf16)
            moved = dot(mask, dy_ref[s])
            din[rows] = moved.astype(bf16)
            gdin[rows] = (moved * gates).astype(bf16)

    wi = wi_ref[0]
    wo = wo_ref[0]
    for s in range(2):
        rows = slice(s * cap, s * cap + cap)
        gates = gcol[rows, 0:1]
        a = dot(xin[rows], wi)
        u = dot(din[rows], wo, 1, 1)
        t = jnp.tanh(ROOT * (a + CUBE * a * a * a))
        act = 0.5 * a * (1.0 + t)
        slope = 0.5 * (1.0 + t) + 0.5 * a * (1.0 - t * t) * (
            ROOT * (1.0 + 3.0 * CUBE * a * a)
        )
        low_act = act.astype(bf16)
        da = (u * gates * slope).astype(bf16)
        dg = jnp.sum(low_act.astype(f32) * u, axis=1, keepdims=True)
        dg_ref[0, s : s + 1, :] += jnp.sum(
            jnp.where(pick[rows] > 0, dg, 0.0), axis=0, keepdims=True
        )
        eo[rows] += dot(low_act, wo)
        dxin[rows] += dot(da, wi, 1, 1)
        left = dot(xin[rows], da, 0, 0)
        right = dot(gdin[rows], low_act, 0, 0)
        if s == 0:
            gsum_i, gsum_o = left, right
        else:
            gi_ref[0] = (gsum_i + left).astype(bf16)
            go_ref[0] = (gsum_o + right).astype(bf16)

    @pl.when(chunk == pl.num_programs(1) - 1)
    def _():
        for s in range(2):
            rows = slice(s * cap, s * cap + cap)
            mask = pick[rows]
            out = (eo[rows] * gcol[rows, 0:1]).astype(bf16)
            y_ref[s] = (y_ref[s].astype(f32) + dot(mask, out, 0, 0)).astype(bf16)
            back = dxin[rows].astype(bf16)
            dx_ref[s] = (dx_ref[s].astype(f32) + dot(mask, back, 0, 0)).astype(bf16)


def moe(x, dy, pos, gate, w_in, w_out, cap):
    experts, d, hidden = w_in.shape
    seq = x.shape[1]
    whole = pl.BlockSpec((2, seq, d), lambda e, c: (0, 0, 0), pipeline_mode=pl.Buffered(1))
    result = pl.BlockSpec((2, seq, d), lambda e, c: (0, 0, 0))
    small = pl.BlockSpec((1, 2, seq), lambda e, c: (e, 0, 0))
    wide = pl.BlockSpec((1, d, CHUNK), lambda e, c: (e, 0, c))
    tall = pl.BlockSpec((1, CHUNK, d), lambda e, c: (e, c, 0))
    return pl.pallas_call(
        functools.partial(moe_kernel, cap),
        grid=(experts, hidden // CHUNK),
        in_specs=[whole, whole, small, small, wide, tall],
        out_specs=[result, result, small, wide, wide],
        out_shape=[
            jax.ShapeDtypeStruct((2, seq, d), bf16),
            jax.ShapeDtypeStruct((2, seq, d), bf16),
            jax.ShapeDtypeStruct((experts, 2, seq), f32),
            jax.ShapeDtypeStruct((experts, d, hidden), bf16),
            jax.ShapeDtypeStruct((experts, d, hidden), bf16),
        ],
        scratch_shapes=[
            pltpu.VMEM((2 * cap, seq), bf16),
            pltpu.VMEM((2 * cap, d), bf16),
            pltpu.VMEM((2 * cap, d), bf16),
            pltpu.VMEM((2 * cap, d), bf16),
            pltpu.VMEM((2 * cap, 128), f32),
            pltpu.VMEM((2 * cap, d), f32),
            pltpu.VMEM((2 * cap, d), f32),
        ],
        compiler_params=pltpu.CompilerParams(vmem_limit_bytes=60 << 20),
    )(x, dy, pos, gate, w_in, w_out)


def swap(x, axis):
    return lax.ppermute(x, axis, [(0, 1), (1, 0)])


def after(x, *others):
    return lax.optimization_barrier((x, *others))[0]


def joined(mine, theirs, index, axis):
    return jnp.where(
        index == 0,
        jnp.concatenate([mine, theirs], axis),
        jnp.concatenate([theirs, mine], axis),
    )


def split(value):
    high = lax.reduce_precision(value, 8, 7)
    return jnp.concatenate([high.astype(bf16), (value - high).astype(bf16)], 0)


def local(
    n_dp,
    tokens, gain_attn, w_query, w_key, w_value, w_output,
    gain_moe, w_router, w_in, w_out, routes, cotangent,
):
    seq, width = tokens.shape
    tensor = lax.axis_index("tensor")
    core = lax.axis_index("expert")
    dp = lax.axis_index("dp")
    experts = w_router.shape[1]
    mine_experts = w_in.shape[0]
    cap = 5 * TOP * seq // (4 * experts)

    other_tokens = swap(tokens, "tensor")
    other_routes = swap(routes, "expert")
    whole_in = joined(tokens, other_tokens, tensor, 1)
    other_cot = swap(after(cotangent, other_tokens), "tensor")
    other_wo = swap(after(w_output, other_cot), "tensor")

    residual = whole_in.astype(f32)
    scale_one = rms_scale(residual)
    normed_one = residual * scale_one
    low_one = (normed_one * gain_attn).astype(bf16)
    query = dot(low_one, w_query).astype(bf16)
    key = dot(low_one, w_key).astype(bf16)
    value = dot(low_one, w_value).astype(bf16)
    heads_out, log_total = attend(query, key, value)
    other_heads = swap(heads_out, "tensor")

    lanes = jnp.arange(experts, dtype=jnp.int32)[:, None]
    earlier = (
        jnp.arange(seq, dtype=jnp.int32)[:, None] < jnp.arange(seq, dtype=jnp.int32)[None, :]
    ).astype(bf16)

    def places(table):
        named = (table[0:1] == lanes) | (table[1:2] == lanes)
        before = dot(named.astype(bf16), earlier).astype(jnp.int32)
        return jnp.where(named, before, -1)

    table, other_table = routes.T, other_routes.T
    first = core * mine_experts
    pos = jnp.stack(
        [
            lax.dynamic_slice_in_dim(places(table), first, mine_experts, 0),
            lax.dynamic_slice_in_dim(places(other_table), first, mine_experts, 0),
        ],
        1,
    )
    whole_cot = joined(cotangent, other_cot, tensor, 1)
    cots = jnp.stack([whole_cot, swap(whole_cot, "expert")])
    grad_top = whole_cot.astype(f32)
    whole_wo = joined(w_output, other_wo, tensor, 0)

    all_heads = joined(heads_out, other_heads, tensor, 1)
    hidden = residual + dot(all_heads, whole_wo)
    scale_two = rms_scale(hidden)
    normed_two = hidden * scale_two
    low_two = (normed_two * gain_moe).astype(bf16)
    logits = dot(w_router, low_two, 0, 1)
    picks = [(table[j : j + 1] == lanes).astype(f32) for j in range(TOP)]
    chosen = jnp.concatenate([jnp.sum(p * logits, 0, keepdims=True) for p in picks], 0)
    expo = jnp.exp(chosen - jnp.max(chosen, 0, keepdims=True))
    gates = expo / jnp.sum(expo, 0, keepdims=True)
    by_expert = picks[0] * gates[0:1] + picks[1] * gates[1:2]
    other_low = swap(low_two, "expert")
    other_gates = swap(by_expert, "expert")
    gate = jnp.stack(
        [
            lax.dynamic_slice_in_dim(by_expert, first, mine_experts, 0),
            lax.dynamic_slice_in_dim(other_gates, first, mine_experts, 0),
        ],
        1,
    )
    y, dx, dg, grad_w_in, grad_w_out = moe(
        jnp.stack([low_two, other_low]), cots, pos, gate, w_in, w_out, cap
    )

    dx_part = (dx[0].astype(f32) + swap(dx[1], "expert").astype(f32)).astype(bf16)
    dg_part = joined(dg[:, 0], swap(dg[:, 1], "expert"), core, 0)
    dx_other = swap(dx_part, "tensor")
    gate_grad = dg_part + swap(dg_part, "tensor")
    grad_two_sum = dx_part.astype(f32) + dx_other.astype(f32)

    def columns(a, index):
        return lax.dynamic_slice_in_dim(a, index * width, width, 1)

    y_part = (y[0].astype(f32) + swap(after(y[1], dx_part), "expert").astype(f32)).astype(bf16)
    y_other = swap(after(columns(y_part, 1 - tensor), dx_other), "tensor")
    mixed = (
        columns(hidden, tensor) + columns(y_part, tensor).astype(f32) + y_other.astype(f32)
    ).astype(bf16)

    outer = n_dp // 2
    share = D // n_dp
    pairs = [(i, i ^ 1) for i in range(n_dp)]
    groups = [list(range(r, n_dp, 2)) for r in range(2)]
    low_bit = lax.rem(dp, 2)
    ffs = w_in.shape[2]

    def pair_sum(a, axis):
        mine = lax.dynamic_index_in_dim(a, low_bit, axis, keepdims=False)
        send = lax.dynamic_index_in_dim(a, 1 - low_bit, axis, keepdims=False)
        return mine.astype(f32) + lax.ppermute(send, "dp", pairs).astype(f32)

    def line_sum(a):
        return lax.psum_scatter(
            a, "dp", scatter_dimension=1, axis_index_groups=groups, tiled=True
        )

    def shares(a):
        return a.reshape(mine_experts, outer, 2, share, ffs)

    out_half = pair_sum(shares(grad_w_out), 2).astype(bf16)
    in_quarter = line_sum(grad_w_in.reshape(mine_experts, outer, 2 * share, ffs))
    out_share = line_sum(out_half).reshape(mine_experts, share, ffs)
    in_share = pair_sum(in_quarter.reshape(mine_experts, 2, share, ffs), 1)
    grad_in_share = in_share
    grad_out_share = jnp.swapaxes(out_share, 1, 2).astype(f32)

    grads_j = [jnp.sum(p * gate_grad, 0, keepdims=True) for p in picks]
    mean_j = gates[0:1] * grads_j[0] + gates[1:2] * grads_j[1]
    grad_logits = sum(picks[j] * (gates[j : j + 1] * (grads_j[j] - mean_j)) for j in range(TOP))
    parts = split(grad_logits)
    grad_two = grad_two_sum + dot(parts, jnp.concatenate([w_router, w_router], 1), 0, 1)
    router_parts = dot(parts, low_two)
    grad_router = (router_parts[:experts] + router_parts[experts:]).T
    grad_gain_moe = jnp.sum(grad_two * normed_two, axis=0)
    scaled_two = grad_two * gain_moe
    grad_hidden = grad_top + scale_two * (
        scaled_two - normed_two * jnp.mean(normed_two * scaled_two, axis=1, keepdims=True)
    )
    grad_attn = grad_hidden.astype(bf16)
    grad_heads = dot(grad_attn, w_output, 1, 1).astype(bf16)
    grad_w_output = dot(heads_out, grad_attn, 0, 0)
    dq, dk, dv = attend_back(query, key, value, heads_out, log_total, grad_heads)
    grad_qkv = [dot(low_one, g, 0, 0) for g in (dq, dk, dv)]
    grad_one = dot(dq, w_query, 1, 1) + dot(dk, w_key, 1, 1) + dot(dv, w_value, 1, 1)
    gain_part = jnp.sum(grad_one * normed_one, axis=0)
    scaled_one = grad_one * gain_attn
    grad_in_part = scale_one * (
        scaled_one - normed_one * jnp.mean(normed_one * scaled_one, axis=1, keepdims=True)
    )
    theirs = swap(columns(grad_in_part, 1 - tensor).astype(bf16), "tensor")
    grad_tokens = (
        columns(grad_hidden, tensor) + columns(grad_in_part, tensor) + theirs.astype(f32)
    )
    dense = jnp.concatenate([g.astype(bf16) for g in grad_qkv], 1)
    dense = lax.psum(
        jnp.concatenate([dense, grad_w_output.astype(bf16).reshape(D, width)], 1),
        ("dp", "expert"),
    ).astype(f32)
    tiny = lax.psum(
        jnp.concatenate([gain_part, 0.5 * grad_gain_moe, 0.5 * grad_router.reshape(-1)]),
        ("dp", "expert", "tensor"),
    )
    return (
        mixed,
        grad_tokens,
        lax.dynamic_slice_in_dim(tiny[:D], tensor * width, width, 0),
        dense[:, :width],
        dense[:, width : 2 * width],
        dense[:, 2 * width : 3 * width],
        dense[:, 3 * width :].reshape(width, D),
        tiny[D : 2 * D],
        tiny[2 * D :].reshape(D, experts),
        grad_in_share,
        grad_out_share,
    )


def solution(mesh):
    in_specs = (
        P(("dp", "expert"), "tensor"),
        P(),
        P(None, "tensor"),
        P(None, "tensor"),
        P(None, "tensor"),
        P("tensor", None),
        P(),
        P(),
        P("expert", None, "tensor"),
        P("expert", "tensor", None),
        P(("dp", "expert"), None),
        P(("dp", "expert"), "tensor"),
    )
    out_specs = (
        P(("dp", "expert"), "tensor"),
        P(("dp", "expert"), "tensor"),
        P("tensor"),
        P(None, "tensor"),
        P(None, "tensor"),
        P(None, "tensor"),
        P("tensor", None),
        P(),
        P(),
        P("expert", "dp", "tensor"),
        P("expert", "tensor", "dp"),
    )
    return jax.shard_map(
        functools.partial(local, mesh.shape["dp"]),
        mesh=mesh,
        in_specs=in_specs,
        out_specs=out_specs,
        check_vma=False,
    )
```

```python
import functools
import math

import jax
import jax.numpy as jnp
from jax import lax
from jax.experimental import pallas as pl
from jax.experimental.pallas import tpu as pltpu
from jax.sharding import PartitionSpec as P

D = 768
DH = 64
TOP = 2
epsilon = 1e-06
bf16 = jnp.bfloat16
f32 = jnp.float32
FACTOR = 1.0 / math.sqrt(DH)
QB = 256
CHUNK = 768
ROOT = math.sqrt(2.0 / math.pi)
CUBE = 0.044715


def rms_scale(rows):
    return lax.rsqrt(jnp.mean(rows * rows, axis=-1, keepdims=True) + epsilon)


def dot(a, b, ca=1, cb=0):
    return lax.dot_general(a, b, (((ca,), (cb,)), ((), ())), preferred_element_type=f32)


def causal(rows, cols, start):
    at = start + lax.broadcasted_iota(jnp.int32, (rows, cols), 0)
    return lax.broadcasted_iota(jnp.int32, (rows, cols), 1) <= at


def attend_kernel(q_ref, k_ref, v_ref, o_ref, l_ref):
    seq = q_ref.shape[0]
    for half in range(2):
        cols = slice(half * DH, half * DH + DH)
        for start in range(0, seq, QB):
            end = start + QB
            s = dot(q_ref[start:end, cols], k_ref[:end, cols], 1, 1) * FACTOR
            s = jnp.where(causal(QB, end, start), s, -1e30)
            peak = jnp.max(s, axis=1, keepdims=True)
            expo = jnp.exp(s - peak)
            total = jnp.sum(expo, axis=1, keepdims=True)
            prob = (expo * (1.0 / total)).astype(bf16)
            o_ref[start:end, cols] = dot(prob, v_ref[:end, cols]).astype(bf16)
            l_ref[start:end, cols] = jnp.broadcast_to(peak + jnp.log(total), (QB, DH))


def attend(query, key, value):
    seq, width = query.shape
    spec = pl.BlockSpec((seq, 128), lambda i: (0, i))
    return pl.pallas_call(
        attend_kernel,
        grid=(width // 128,),
        in_specs=[spec] * 3,
        out_specs=[spec] * 2,
        out_shape=[
            jax.ShapeDtypeStruct((seq, width), bf16),
            jax.ShapeDtypeStruct((seq, width), f32),
        ],
        compiler_params=pltpu.CompilerParams(vmem_limit_bytes=48 << 20),
    )(query, key, value)


def back_kernel(q_ref, k_ref, v_ref, o_ref, l_ref, g_ref, dq_ref, dk_ref, dv_ref, ks, vs):
    seq = q_ref.shape[0]
    for half in range(2):
        cols = slice(half * DH, half * DH + DH)
        ks[...] = jnp.zeros_like(ks)
        vs[...] = jnp.zeros_like(vs)
        for start in range(0, seq, QB):
            end = start + QB
            q = q_ref[start:end, cols]
            k = k_ref[:end, cols]
            g = g_ref[start:end, cols]
            s = dot(q, k, 1, 1) * FACTOR
            log_total = l_ref[start:end, half * DH : half * DH + 1]
            prob = jnp.where(causal(QB, end, start), jnp.exp(s - log_total), 0.0)
            gp = dot(g, v_ref[:end, cols], 1, 1)
            inner = jnp.sum(
                g.astype(f32) * o_ref[start:end, cols].astype(f32), axis=1, keepdims=True
            )
            ds = (prob * (gp - inner)).astype(bf16)
            dq_ref[start:end, cols] = (dot(ds, k) * FACTOR).astype(bf16)
            ks[:end] += dot(ds, q, 0, 0)
            vs[:end] += dot(prob.astype(bf16), g, 0, 0)
        dk_ref[:, cols] = (ks[...] * FACTOR).astype(bf16)
        dv_ref[:, cols] = vs[...].astype(bf16)


def attend_back(query, key, value, out, log_total, grad):
    seq, width = query.shape
    spec = pl.BlockSpec((seq, 128), lambda i: (0, i))
    return pl.pallas_call(
        back_kernel,
        grid=(width // 128,),
        in_specs=[spec] * 6,
        out_specs=[spec] * 3,
        out_shape=[jax.ShapeDtypeStruct((seq, width), bf16)] * 3,
        scratch_shapes=[pltpu.VMEM((seq, DH), f32)] * 2,
        compiler_params=pltpu.CompilerParams(vmem_limit_bytes=48 << 20),
    )(query, key, value, out, log_total, grad)


def moe_kernel(
    cap,
    x_ref, dy_ref, pos_ref, gate_ref, wi_ref, wo_ref,
    y_ref, dx_ref, dg_ref, gi_ref, go_ref,
    pick, xin, din, gdin, gcol, eo, dxin,
):
    expert, chunk = pl.program_id(0), pl.program_id(1)
    seq = x_ref.shape[1]

    @pl.when((expert == 0) & (chunk == 0))
    def _():
        y_ref[...] = jnp.zeros_like(y_ref)
        dx_ref[...] = jnp.zeros_like(dx_ref)

    @pl.when(chunk == 0)
    def _():
        dg_ref[...] = jnp.zeros_like(dg_ref)
        eo[...] = jnp.zeros_like(eo)
        dxin[...] = jnp.zeros_like(dxin)
        for s in range(2):
            rows = slice(s * cap, s * cap + cap)
            hit = lax.broadcasted_iota(jnp.int32, (cap, seq), 0) == pos_ref[0, s : s + 1, :]
            gates = jnp.sum(
                jnp.where(hit, gate_ref[0, s : s + 1, :], 0.0), axis=1, keepdims=True
            )
            gcol[rows] = jnp.broadcast_to(gates, (cap, 128))
            mask = jnp.where(hit, 1.0, 0.0).astype(bf16)
            pick[rows] = mask
            xin[rows] = dot(mask, x_ref[s]).astype(bf16)
            moved = dot(mask, dy_ref[s])
            din[rows] = moved.astype(bf16)
            gdin[rows] = (moved * gates).astype(bf16)

    wi = wi_ref[0]
    wo = wo_ref[0]
    for s in range(2):
        rows = slice(s * cap, s * cap + cap)
        gates = gcol[rows, 0:1]
        a = dot(xin[rows], wi)
        u = dot(din[rows], wo, 1, 1)
        t = jnp.tanh(ROOT * (a + CUBE * a * a * a))
        act = 0.5 * a * (1.0 + t)
        slope = 0.5 * (1.0 + t) + 0.5 * a * (1.0 - t * t) * (
            ROOT * (1.0 + 3.0 * CUBE * a * a)
        )
        low_act = act.astype(bf16)
        da = (u * gates * slope).astype(bf16)
        dg = jnp.sum(low_act.astype(f32) * u, axis=1, keepdims=True)
        dg_ref[0, s : s + 1, :] += jnp.sum(
            jnp.where(pick[rows] > 0, dg, 0.0), axis=0, keepdims=True
        )
        eo[rows] += dot(low_act, wo)
        dxin[rows] += dot(da, wi, 1, 1)
        left = dot(xin[rows], da, 0, 0)
        right = dot(gdin[rows], low_act, 0, 0)
        if s == 0:
            gsum_i, gsum_o = left, right
        else:
            tile = (gi_ref.shape[0],) + gi_ref.shape[2:]
            gi_ref[:, 0] = (gsum_i + left).astype(bf16).reshape(tile)
            go_ref[:, 0] = (gsum_o + right).astype(bf16).reshape(tile)

    @pl.when(chunk == pl.num_programs(1) - 1)
    def _():
        for s in range(2):
            rows = slice(s * cap, s * cap + cap)
            mask = pick[rows]
            out = (eo[rows] * gcol[rows, 0:1]).astype(bf16)
            y_ref[s] = (y_ref[s].astype(f32) + dot(mask, out, 0, 0)).astype(bf16)
            back = dxin[rows].astype(bf16)
            dx_ref[s] = (dx_ref[s].astype(f32) + dot(mask, back, 0, 0)).astype(bf16)


def moe(x, dy, pos, gate, w_in, w_out, cap, begin, experts, outer):
    _, d, hidden = w_in.shape
    split_rows = d // outer
    seq = x.shape[1]
    whole = pl.BlockSpec((2, seq, d), lambda e, c: (0, 0, 0), pipeline_mode=pl.Buffered(1))
    result = pl.BlockSpec((2, seq, d), lambda e, c: (0, 0, 0))
    small = pl.BlockSpec((1, 2, seq), lambda e, c: (begin + e, 0, 0))
    wide = pl.BlockSpec((1, d, CHUNK), lambda e, c: (begin + e, 0, c))
    tall = pl.BlockSpec((1, CHUNK, d), lambda e, c: (begin + e, c, 0))
    small_out = pl.BlockSpec((1, 2, seq), lambda e, c: (e, 0, 0))
    graded = pl.BlockSpec((outer, 1, split_rows, CHUNK), lambda e, c: (0, e, 0, c))
    return pl.pallas_call(
        functools.partial(moe_kernel, cap),
        grid=(experts, hidden // CHUNK),
        in_specs=[whole, whole, small, small, wide, tall],
        out_specs=[result, result, small_out, graded, graded],
        out_shape=[
            jax.ShapeDtypeStruct((2, seq, d), bf16),
            jax.ShapeDtypeStruct((2, seq, d), bf16),
            jax.ShapeDtypeStruct((experts, 2, seq), f32),
            jax.ShapeDtypeStruct((outer, experts, split_rows, hidden), bf16),
            jax.ShapeDtypeStruct((outer, experts, split_rows, hidden), bf16),
        ],
        scratch_shapes=[
            pltpu.VMEM((2 * cap, seq), bf16),
            pltpu.VMEM((2 * cap, d), bf16),
            pltpu.VMEM((2 * cap, d), bf16),
            pltpu.VMEM((2 * cap, d), bf16),
            pltpu.VMEM((2 * cap, 128), f32),
            pltpu.VMEM((2 * cap, d), f32),
            pltpu.VMEM((2 * cap, d), f32),
        ],
        compiler_params=pltpu.CompilerParams(vmem_limit_bytes=60 << 20),
    )(x, dy, pos, gate, w_in, w_out)


def swap(x, axis):
    return lax.ppermute(x, axis, [(0, 1), (1, 0)])


def after(x, *others):
    return lax.optimization_barrier((x, *others))[0]


def joined(mine, theirs, index, axis):
    return jnp.where(
        index == 0,
        jnp.concatenate([mine, theirs], axis),
        jnp.concatenate([theirs, mine], axis),
    )


def split(value):
    high = lax.reduce_precision(value, 8, 7)
    return jnp.concatenate([high.astype(bf16), (value - high).astype(bf16)], 0)


def local(
    n_dp,
    tokens, gain_attn, w_query, w_key, w_value, w_output,
    gain_moe, w_router, w_in, w_out, routes, cotangent,
):
    seq, width = tokens.shape
    tensor = lax.axis_index("tensor")
    core = lax.axis_index("expert")
    dp = lax.axis_index("dp")
    experts = w_router.shape[1]
    mine_experts = w_in.shape[0]
    cap = 5 * TOP * seq // (4 * experts)

    other_tokens = swap(tokens, "tensor")
    other_routes = swap(routes, "expert")
    whole_in = joined(tokens, other_tokens, tensor, 1)
    other_cot = swap(after(cotangent, other_tokens), "tensor")
    other_wo = swap(after(w_output, other_cot), "tensor")

    residual = whole_in.astype(f32)
    scale_one = rms_scale(residual)
    normed_one = residual * scale_one
    low_one = (normed_one * gain_attn).astype(bf16)
    query = dot(low_one, w_query).astype(bf16)
    key = dot(low_one, w_key).astype(bf16)
    value = dot(low_one, w_value).astype(bf16)
    heads_out, log_total = attend(query, key, value)
    other_heads = swap(heads_out, "tensor")

    lanes = jnp.arange(experts, dtype=jnp.int32)[:, None]
    earlier = (
        jnp.arange(seq, dtype=jnp.int32)[:, None] < jnp.arange(seq, dtype=jnp.int32)[None, :]
    ).astype(bf16)

    def places(table):
        named = (table[0:1] == lanes) | (table[1:2] == lanes)
        before = dot(named.astype(bf16), earlier).astype(jnp.int32)
        return jnp.where(named, before, -1)

    table, other_table = routes.T, other_routes.T
    first = core * mine_experts
    pos = jnp.stack(
        [
            lax.dynamic_slice_in_dim(places(table), first, mine_experts, 0),
            lax.dynamic_slice_in_dim(places(other_table), first, mine_experts, 0),
        ],
        1,
    )
    whole_cot = joined(cotangent, other_cot, tensor, 1)
    cots = jnp.stack([whole_cot, swap(whole_cot, "expert")])
    grad_top = whole_cot.astype(f32)
    whole_wo = joined(w_output, other_wo, tensor, 0)

    all_heads = joined(heads_out, other_heads, tensor, 1)
    hidden = residual + dot(all_heads, whole_wo)
    scale_two = rms_scale(hidden)
    normed_two = hidden * scale_two
    low_two = (normed_two * gain_moe).astype(bf16)
    logits = dot(w_router, low_two, 0, 1)
    picks = [(table[j : j + 1] == lanes).astype(f32) for j in range(TOP)]
    chosen = jnp.concatenate([jnp.sum(p * logits, 0, keepdims=True) for p in picks], 0)
    expo = jnp.exp(chosen - jnp.max(chosen, 0, keepdims=True))
    gates = expo / jnp.sum(expo, 0, keepdims=True)
    by_expert = picks[0] * gates[0:1] + picks[1] * gates[1:2]
    other_low = swap(low_two, "expert")
    other_gates = swap(by_expert, "expert")
    gate = jnp.stack(
        [
            lax.dynamic_slice_in_dim(by_expert, first, mine_experts, 0),
            lax.dynamic_slice_in_dim(other_gates, first, mine_experts, 0),
        ],
        1,
    )
    outer = n_dp // 2
    share = D // n_dp
    pairs = [(i, i ^ 1) for i in range(n_dp)]
    groups = [list(range(r, n_dp, 2)) for r in range(2)]
    low_bit = lax.rem(dp, 2)
    ffs = w_in.shape[2]
    some = mine_experts // 2

    def halves(a):
        a = a.reshape(a.shape[0], some, 2, share, ffs)
        mine = lax.dynamic_index_in_dim(a, low_bit, 2, keepdims=False)
        return mine, lax.dynamic_index_in_dim(a, 1 - low_bit, 2, keepdims=False)

    def pair(send):
        return lax.ppermute(send, "dp", pairs).astype(f32)

    def line_sum(a):
        return lax.psum_scatter(
            a, "dp", scatter_dimension=0, axis_index_groups=groups, tiled=True
        )

    both = jnp.stack([low_two, other_low])
    y_a, dx_a, dg_a, gi_a, go_a = moe(
        both, cots, pos, gate, w_in, w_out, cap, 0, some, outer
    )
    go_a_mine, go_a_send = halves(go_a)
    gi_a_line = line_sum(gi_a)
    y_b, dx_b, dg_b, gi_b, go_b = moe(
        after(both, go_a_send), cots, pos, gate, w_in, w_out, cap, some, some, outer
    )
    go_a_pair = pair(go_a_send)

    dx_part = (
        dx_a[0].astype(f32)
        + dx_b[0].astype(f32)
        + swap(dx_a[1], "expert").astype(f32)
        + swap(dx_b[1], "expert").astype(f32)
    ).astype(bf16)
    dg = jnp.concatenate([dg_a, dg_b], 0)
    dg_part = joined(dg[:, 0], swap(dg[:, 1], "expert"), core, 0)
    dx_other = swap(dx_part, "tensor")
    gate_grad = dg_part + swap(dg_part, "tensor")
    grad_two_sum = dx_part.astype(f32) + dx_other.astype(f32)

    gi_b, go_b = lax.optimization_barrier((gi_b, go_b, dx_part))[:2]
    gi_b_mine, gi_b_send = halves(gi_b)
    go_b_mine, go_b_send = halves(go_b)
    gi_b_pair = pair(after(gi_b_send, go_a_pair))
    go_a_half = (go_a_mine.astype(f32) + go_a_pair).astype(bf16)
    go_a_line = line_sum(go_a_half)
    go_b_pair = pair(after(go_b_send, gi_b_pair))
    gi_b_line = line_sum((gi_b_mine.astype(f32) + gi_b_pair).astype(bf16))
    go_b_half = (go_b_mine.astype(f32) + go_b_pair).astype(bf16)
    go_b_line = line_sum(go_b_half)

    def columns(a, index):
        return lax.dynamic_slice_in_dim(a, index * width, width, 1)

    y_part = (
        y_a[0].astype(f32)
        + y_b[0].astype(f32)
        + swap(y_a[1], "expert").astype(f32)
        + swap(after(y_b[1], dx_part), "expert").astype(f32)
    ).astype(bf16)
    y_other = swap(after(columns(y_part, 1 - tensor), dx_other), "tensor")
    mixed = (
        columns(hidden, tensor) + columns(y_part, tensor).astype(f32) + y_other.astype(f32)
    ).astype(bf16)

    grads_j = [jnp.sum(p * gate_grad, 0, keepdims=True) for p in picks]
    mean_j = gates[0:1] * grads_j[0] + gates[1:2] * grads_j[1]
    grad_logits = sum(picks[j] * (gates[j : j + 1] * (grads_j[j] - mean_j)) for j in range(TOP))
    parts = split(grad_logits)
    grad_two = grad_two_sum + dot(parts, jnp.concatenate([w_router, w_router], 1), 0, 1)
    router_parts = dot(parts, low_two)
    grad_router = (router_parts[:experts] + router_parts[experts:]).T
    grad_gain_moe = jnp.sum(grad_two * normed_two, axis=0)
    scaled_two = grad_two * gain_moe
    grad_hidden = grad_top + scale_two * (
        scaled_two - normed_two * jnp.mean(normed_two * scaled_two, axis=1, keepdims=True)
    )
    grad_attn = grad_hidden.astype(bf16)
    grad_heads = dot(grad_attn, w_output, 1, 1).astype(bf16)
    grad_w_output = dot(heads_out, grad_attn, 0, 0)
    dq, dk, dv = attend_back(query, key, value, heads_out, log_total, grad_heads)
    grad_qkv = [dot(low_one, g, 0, 0) for g in (dq, dk, dv)]
    grad_one = dot(dq, w_query, 1, 1) + dot(dk, w_key, 1, 1) + dot(dv, w_value, 1, 1)
    gain_part = jnp.sum(grad_one * normed_one, axis=0)
    scaled_one = grad_one * gain_attn
    grad_in_part = scale_one * (
        scaled_one - normed_one * jnp.mean(normed_one * scaled_one, axis=1, keepdims=True)
    )
    theirs = swap(columns(grad_in_part, 1 - tensor).astype(bf16), "tensor")
    grad_tokens = (
        columns(grad_hidden, tensor) + columns(grad_in_part, tensor) + theirs.astype(f32)
    )
    gain_row = gain_part[None]
    gain_share = columns(gain_row, tensor) + swap(columns(gain_row, 1 - tensor), "tensor")
    tiny = jnp.concatenate([gain_share[0], grad_gain_moe, grad_router.reshape(-1)])
    grad_qkv[2] = jnp.concatenate([grad_qkv[2], tiny.reshape(-1, width)], 0)
    dense = [g.astype(bf16) for g in grad_qkv + [grad_w_output]]
    dense = lax.optimization_barrier((*dense, go_b_half))[:-1]
    dense = [g.astype(f32) for g in lax.psum(dense, ("dp", "expert"))]
    tiny = dense[2][D:].reshape(-1)

    gi_a_mine, gi_a_send = halves(gi_a_line)
    gi_a_share = (gi_a_mine.astype(f32) + pair(gi_a_send))[0]
    grad_in_share = jnp.concatenate([gi_a_share, gi_b_line[0].astype(f32)], 0)
    grad_out_share = jnp.concatenate([go_a_line[0], go_b_line[0]], 0)
    grad_out_share = jnp.swapaxes(grad_out_share, 1, 2).astype(f32)
    return (
        mixed,
        grad_tokens,
        tiny[:width],
        dense[0],
        dense[1],
        dense[2][:D],
        dense[3],
        tiny[width : width + D],
        tiny[width + D :].reshape(D, experts),
        grad_in_share,
        grad_out_share,
    )


def solution(mesh):
    in_specs = (
        P(("dp", "expert"), "tensor"),
        P(),
        P(None, "tensor"),
        P(None, "tensor"),
        P(None, "tensor"),
        P("tensor", None),
        P(),
        P(),
        P("expert", None, "tensor"),
        P("expert", "tensor", None),
        P(("dp", "expert"), None),
        P(("dp", "expert"), "tensor"),
    )
    out_specs = (
        P(("dp", "expert"), "tensor"),
        P(("dp", "expert"), "tensor"),
        P("tensor"),
        P(None, "tensor"),
        P(None, "tensor"),
        P(None, "tensor"),
        P("tensor", None),
        P(),
        P(),
        P("expert", "dp", "tensor"),
        P("expert", "tensor", "dp"),
    )
    return jax.shard_map(
        functools.partial(local, mesh.shape["dp"]),
        mesh=mesh,
        in_specs=in_specs,
        out_specs=out_specs,
        check_vma=False,
    )
```
